256 devices in a mesh: row: 64 (over y_hi, x, z), head: 4 (over y_lo, core).
Axes of the slice: x: 4, y: 4 (y_hi: 2, y_lo: 2; y = y_hi * 2 + y_lo), z: 8, core: 2. Of those that a mesh axis runs over, the one named last changes fastest.
Arguments:
- pair: float32 [1024, 1024, 128], P('row', 'head'), may hold values from -6 to 6
- token_mask: int32 [1024], replicated, may hold values from 0 to 1, as said below
- ln_gain: float32 [128], replicated, may hold values from 0.25 to 1.75
- ln_shift: float32 [128], replicated, may hold values from -3 to 3
- w_qkvg: bfloat16 [128, 512], P(None, 'head'), may hold values from -0.5 to 0.5
- w_bias: bfloat16 [128, 4], replicated, may hold values from -0.5 to 0.5
- gate_shift: float32 [128], P('head'), may hold values from -4 to 4
- w_out: bfloat16 [128, 128], P('head'), may hold values from -0.5 to 0.5
- out_shift: float32 [128], replicated, may hold values from -4 to 4
Outputs:
- update: float32 [1024, 1024, 128], P('row', 'head')
The draws below stay inside these ranges and needn't reach their ends.
Inputs may be any that keep to these rules, and one draw needn't show every extreme that they name: `token_mask`: 1 for the first tokens and 0 for the rest, with at least 512 ones and at least one 0.
All inputs are finite; a program needn't handle non-finite values.
Results may differ from the reference program's by a relative error of at most 0.0055.
Values may be sent and summed in bfloat16 or wider, within the bound.
No kernel may reach another device: no remote copies, remote signals or barrier semaphores. Data moves between devices by JAX's collectives and lax.ppermute only.
A program may use at most 64 MiB of HBM per device.

```python
import math
import jax
import jax.numpy as jnp
from jax import lax

C = 128
H = 4
DH = 32
N = 1024


def draw_token_mask(key, part):
    key = jax.random.fold_in(key, 7)
    length = jax.random.randint(key, (), N // 2, N)
    return (jnp.arange(N) < length).astype(jnp.int32)


def level_of(rng, shape, pieces, low, high):
    def one(position, shards_of):
        heights = jax.random.uniform(jax.random.fold_in(jax.random.fold_in(rng, 6), position), (shards_of,), jnp.float32, low / len(pieces), high / len(pieces))
        return jnp.repeat(jnp.exp(heights), shape[position] // shards_of).reshape((-1,) + (1,) * (len(shape) - position - 1))

    factor_of = one(*pieces[0])
    for cut in pieces[1:]:
        factor_of = factor_of * one(*cut)
    return factor_of


def bell_draw(key, shape, spread, reach, cuts=(), dtype=jnp.bfloat16):
    level = level_of(key, shape, cuts, -0.22, 0.18) if cuts else 1.0
    values = jax.random.normal(key, shape, jnp.float32) * spread * level
    return jnp.minimum(jnp.maximum(values, -reach), reach).astype(dtype)


def setup_inputs(seed: int = 0) -> dict:
    streams_of = jax.random.split(jax.random.key(seed), 10)
    return {
        "pair": bell_draw(streams_of[0], (N, N, C), 1.0, 6.0, ((0, 64), (1, 4)), jnp.float32),
        "token_mask": draw_token_mask(jax.random.fold_in(streams_of[9], 71), 0),
        "ln_gain": jnp.clip(1.0 + 0.15 * jax.random.normal(streams_of[2], (C,), jnp.float32), 0.25, 1.75),
        "ln_shift": bell_draw(streams_of[3], (C,), 0.5, 3.0, (), jnp.float32),
        "w_qkvg": bell_draw(streams_of[4], (C, H * 4 * DH), C ** -0.5, 0.5, ((1, 4),)),
        "w_bias": bell_draw(streams_of[5], (C, H), C ** -0.5, 0.5),
        "gate_shift": bell_draw(streams_of[6], (H * DH,), 1.0, 4.0, ((0, 4),), jnp.float32),
        "w_out": bell_draw(streams_of[7], (H * DH, C), (H * DH) ** -0.5, 0.5, ((0, 4),)),
        "out_shift": bell_draw(streams_of[8], (C,), 1.0, 4.0, (), jnp.float32),
    }


def layer_norm(values, gain, shift):
    mean = lax.optimization_barrier(jnp.mean(values, axis=-1, keepdims=True))
    centered = values - mean
    var = lax.optimization_barrier(jnp.mean(centered * centered, axis=-1, keepdims=True))
    return centered / jnp.sqrt(var + 1e-05) * gain + shift

def reference(pair, token_mask, ln_gain, ln_shift, w_qkvg, w_bias, gate_shift, w_out, out_shift):
    normed = layer_norm(pair, ln_gain, ln_shift).astype(jnp.bfloat16)

    def bias_row(row_vals):
        return jnp.dot(row_vals, w_bias, preferred_element_type=jnp.float32)
    bias = jnp.transpose(lax.map(bias_row, normed), (2, 0, 1)).astype(jnp.bfloat16)
    bias_wide = bias.astype(jnp.float32)
    key_add = jnp.where(token_mask == 1, 0.0, -1000000000.0).astype(jnp.float32)
    block = math.gcd(N, 4)
    scale = 1.0 / math.sqrt(DH)
    shift_heads = gate_shift.reshape(H, DH)

    def row_block(rows_in):
        proj = jnp.dot(rows_in.reshape(-1, C), w_qkvg, preferred_element_type=jnp.float32)
        proj = proj.astype(jnp.bfloat16).reshape(block, N, H, 4, DH)
        query = proj[:, :, :, 0, :].astype(jnp.float32)
        keys = proj[:, :, :, 1, :].astype(jnp.float32)
        values = proj[:, :, :, 2, :].astype(jnp.float32)
        gate_raw = proj[:, :, :, 3, :].astype(jnp.float32)
        scores = jnp.einsum('ijhc,ikhc->ihjk', query, keys) * scale + bias_wide[None] + key_add
        weights = jax.nn.softmax(scores, axis=-1).astype(jnp.bfloat16)
        attended = jnp.einsum('ihjk,ikhc->ijhc', weights.astype(jnp.float32), values)
        gated = (jax.nn.sigmoid(gate_raw + shift_heads) * attended).astype(jnp.bfloat16)
        result = jnp.dot(gated.reshape(-1, H * DH), w_out, preferred_element_type=jnp.float32)
        return result.reshape(block, N, C) + out_shift
    blocks = lax.map(row_block, normed.reshape(N // block, block, N, C))
    return blocks.reshape(N, N, C)
```

```python
import functools
import math

import jax
import jax.numpy as jnp
import numpy as np
from jax import lax
from jax.experimental import pallas as pl
from jax.experimental.pallas import tpu as pltpu
from jax.sharding import PartitionSpec as P

bf16 = jnp.bfloat16
f32 = jnp.float32
LOG2E = math.log2(math.e)
LIMIT = 80.0
VMEM = 48 * 2**20
DIMS = (2, 2, 2, 2, 4, 2, 2)


def dot(a, b):
    return jnp.dot(a, b, preferred_element_type=f32)


def dot_nt(a, b):
    return lax.dot_general(a, b, (((1,), (1,)), ((), ())), preferred_element_type=f32)


def send(value, where):
    pairs = []
    for index in range(256):
        spot = [int(v) for v in np.unravel_index(index, DIMS)]
        pairs.append((index, int(np.ravel_multi_index(where(*spot), DIMS))))
    return lax.ppermute(value, ("row", "head"), pairs)


def to_core(yh, xh, xl, zh, zl, yl, c):
    return yh, xh, xl, zh, zl, yl, 1 - c


def to_chip(yh, xh, xl, zh, zl, yl, c):
    return yh, xh, xl, zh, zl, 1 - yl, c


def to_both(yh, xh, xl, zh, zl, yl, c):
    return yh, xh, xl, zh, zl, 1 - yl, 1 - c


def spread(dy, dz):
    def where(yh, xh, xl, zh, zl, yl, c):
        return yl ^ dy, c, xl, zh ^ dz, zl, yh, xh

    return where


def along_z(step):
    def where(yh, xh, xl, zh, zl, yl, c):
        z = (zh * 4 + zl + step) % 8
        return yh, xh, xl, z // 4, z % 4, yl, c

    return where


def along_x(step):
    def where(yh, xh, xl, zh, zl, yl, c):
        x = (xh * 2 + xl + step) % 4
        return yh, x // 2, x % 2, zh, zl, yl, c

    return where


def norm_kernel(pair, gain, shift, wb, normed, chunk, rows):
    step = pl.program_id(0)
    count = pair.shape[0]
    x = pair[...]
    mean = jnp.mean(x, axis=-1, keepdims=True)
    centered = x - mean
    var = jnp.mean(centered * centered, axis=-1, keepdims=True)
    n = (centered * lax.rsqrt(var + 1e-05) * gain[...] + shift[...]).astype(bf16)
    normed[...] = n
    for ii in range(count):
        t = dot_nt(wb[...], n[ii])
        for h in range(4):
            rows[h, pl.ds(step * count + ii, 1), :] = t[h : h + 1]

    @pl.when(step == pl.num_programs(0) - 1)
    def _():
        chunk[...] = rows[...].astype(bf16)


def norm_call(pair, gain, shift, wb):
    n, cols, chans = pair.shape
    per = 4
    return pl.pallas_call(
        norm_kernel,
        grid=(n // per,),
        in_specs=[
            pl.BlockSpec((per, cols, chans), lambda i: (i, 0, 0)),
            pl.BlockSpec((1, chans), lambda i: (0, 0)),
            pl.BlockSpec((1, chans), lambda i: (0, 0)),
            pl.BlockSpec((16, chans), lambda i: (0, 0)),
        ],
        out_specs=[
            pl.BlockSpec((per, cols, chans), lambda i: (i, 0, 0)),
            pl.BlockSpec((4, n, cols), lambda i: (0, 0, 0)),
        ],
        out_shape=[
            jax.ShapeDtypeStruct((n, cols, chans), bf16),
            jax.ShapeDtypeStruct((4, n, cols), bf16),
        ],
        scratch_shapes=[pltpu.VMEM((4, n, cols), f32)],
        compiler_params=pltpu.CompilerParams(vmem_limit_bytes=VMEM),
        cost_estimate=pl.CostEstimate(flops=2 * n * cols * chans * 8, bytes_accessed=4 * 2**20, transcendentals=0),
        name="norm",
    )(pair, gain, shift, wb)


def proj_kernel(first, xa, xb, w0, w1, w2, w3, *rest):
    if first:
        q_out, sg_out, wo_out, kt_out, v_out, bound, wk_s, wv_s, wq_s, wg_s, gs_s = rest
    else:
        q_in, kt_out, v_out, bound, wk_s, wv_s = rest
    ws = (w0, w1, w2, w3)
    width = 32
    scale = LOG2E / math.sqrt(width)

    @pl.when(pl.program_id(0) == 0)
    def _():
        wts = [w[0:128].astype(f32).T for w in ws]

        def rows(kind):
            return jnp.concatenate([t[kind * width : (kind + 1) * width] for t in wts], axis=0)

        wk_s[...] = rows(1).astype(bf16)
        wv_s[...] = rows(2).T.astype(bf16)
        bound[...] = jnp.zeros_like(bound)
        if first:
            wq_s[...] = rows(0).T.astype(bf16)
            wg_s[...] = rows(3).T.astype(bf16)
            wo_out[...] = jnp.concatenate([w[128:160] for w in ws], axis=0)
            lane = lax.broadcasted_iota(jnp.int32, (1, 128), 1) // width
            total = jnp.zeros((1, 128), f32)
            for h, w in enumerate(ws):
                piece = jnp.sum(w[160:176].astype(f32), axis=0, keepdims=True)
                total = jnp.where(lane == h, piece, total)
            gs_s[...] = jnp.broadcast_to(total, gs_s.shape)

    row = lax.broadcasted_iota(jnp.int32, (128, 128), 0) // width
    col = lax.broadcasted_iota(jnp.int32, (128, 128), 1)
    best = bound[...]
    for ii in range(xa.shape[0]):
        if first:
            q = (dot(xa[ii], wq_s[...]) * scale).astype(bf16)
            q_out[ii] = q
            raw = dot(xa[ii], wg_s[...]).astype(bf16).astype(f32)
            sg_out[ii] = jax.nn.sigmoid(raw + gs_s[0:1])
        else:
            q = q_in[ii]
        high = jnp.zeros((128, 1), f32)
        for t, x in enumerate((xa, xb)):
            kt = dot_nt(wk_s[...], x[ii])
            kt_out[ii, t] = kt.astype(bf16)
            high = jnp.maximum(high, jnp.max(jnp.abs(kt), axis=1, keepdims=True))
            v_out[ii, t] = dot(x[ii], wv_s[...]).astype(bf16)
        spread_k = jnp.where(row == col, high, 0.0).astype(bf16)
        most = dot(jnp.abs(q), spread_k)
        best = jnp.maximum(best, jnp.max(most, axis=0, keepdims=True))
    bound[...] = best


def proj_call(first, xa, xb, ws, q=None):
    n, cols, chans = xa.shape
    per = 4
    block = pl.BlockSpec((per, cols, chans), lambda i: (i, 0, 0))

    def whole(*shape):
        return pl.BlockSpec(shape, lambda i: (0,) * len(shape))

    in_specs = [block, block] + [whole(176, 128)] * 4
    args = [xa, xb, *ws]
    out_specs = [
        pl.BlockSpec((per, 2, chans, cols), lambda i: (i, 0, 0, 0)),
        pl.BlockSpec((per, 2, cols, chans), lambda i: (i, 0, 0, 0)),
        whole(8, 128),
    ]
    out_shape = [
        jax.ShapeDtypeStruct((n, 2, chans, cols), bf16),
        jax.ShapeDtypeStruct((n, 2, cols, chans), bf16),
        jax.ShapeDtypeStruct((8, 128), f32),
    ]
    scratch = [pltpu.VMEM((128, 128), bf16)] * 2
    if first:
        out_specs = [block, block, whole(128, 128)] + out_specs
        out_shape = [
            jax.ShapeDtypeStruct((n, cols, chans), bf16),
            jax.ShapeDtypeStruct((n, cols, chans), f32),
            jax.ShapeDtypeStruct((128, 128), bf16),
        ] + out_shape
        scratch = scratch + [pltpu.VMEM((128, 128), bf16)] * 2 + [pltpu.VMEM((8, 128), f32)]
    else:
        in_specs.append(block)
        args.append(q)
    return pl.pallas_call(
        functools.partial(proj_kernel, first),
        grid=(n // per,),
        in_specs=in_specs,
        out_specs=out_specs,
        out_shape=out_shape,
        scratch_shapes=scratch,
        compiler_params=pltpu.CompilerParams(vmem_limit_bytes=VMEM),
        cost_estimate=pl.CostEstimate(
            flops=2 * n * cols * 2 * 128 * 512, bytes_accessed=10 * 2**20, transcendentals=n * cols * 128
        ),
        name="proj_near" if first else "proj_far",
    )(*args)


def attend_kernel(parts, sc, q, kt_a, kt_b, v_a, v_b, sg, wo, osh, keys, near, far, *rest):
    blocks = rest[: len(parts)]
    out, bias, flag = rest[-3:]
    half = q.shape[1]
    member, yh, z = sc[1], sc[2], sc[3]

    @pl.when(pl.program_id(0) == 0)
    def _():
        most = jnp.zeros((16, 256), f32)
        for block, (place, first_slot) in zip(blocks, parts):
            core = sc[place]
            for slot in range(block.shape[0]):
                zs = (z + (8, 7, 9, 6)[slot + first_slot]) % 8
                for dy in range(2):
                    quarter = (((yh ^ dy) * 2) + core) ^ member
                    for dz in range(2):
                        at = pl.multiple_of((zs ^ (4 * dz)) * 16, 16)
                        for h in range(4):
                            value = block[slot, dy, dz, h].astype(f32) * LOG2E
                            most = jnp.maximum(most, jnp.abs(value))
                            bias[quarter, h ^ member, pl.ds(at, 16), :] = value + keys[quarter]
        reach = jnp.max(most) + jnp.max(jnp.maximum(near[...], far[...]))
        flag[0] = (reach < LIMIT).astype(jnp.int32)

    lane = lax.broadcasted_iota(jnp.int32, (half, 128), 1) // 32
    ones = jnp.ones((256, 128), bf16)

    def keys_of(r):
        return (kt_a, kt_b)[r // 2][0, r % 2]

    def values_of(r):
        return jnp.concatenate([(v_a, v_b)[r // 2][0, r % 2], ones], axis=1)

    def finish(pieces):
        att = jnp.zeros((half, 128), f32)
        for h in range(4):
            att = jnp.where(lane == h, pieces[h][:, :128] / pieces[h][:, 128:], att)
        gated = (att * sg[0]).astype(bf16)
        out[0] = dot(gated, wo[...]) + osh[...]

    def query(h):
        return jnp.where(lane == h, q[0], jnp.zeros_like(q[0]))

    @pl.when(flag[0] == 1)
    def _():
        wide = jnp.concatenate([query(h) for h in range(4)], axis=0)
        acc = None
        for r in range(4):
            s = dot(wide, keys_of(r)) + bias[r].reshape(4 * half, 256)
            p = jnp.exp2(s).astype(bf16)
            part = dot(p, values_of(r))
            acc = part if acc is None else acc + part
        finish([acc[h * half : (h + 1) * half] for h in range(4)])

    @pl.when(flag[0] != 1)
    def _():
        pieces = []
        for h in range(4):
            s = [dot(query(h), keys_of(r)) + bias[r, h] for r in range(4)]
            top = functools.reduce(jnp.maximum, [jnp.max(t, axis=1, keepdims=True) for t in s])
            pieces.append(sum(dot(jnp.exp2(s[r] - top).astype(bf16), values_of(r)) for r in range(4)))
        finish(pieces)


def attend_call(parts, sc, q, kts, vs, sg, wo, osh, keys, bounds, blocks, before, name):
    n, cols, chans = q.shape
    half = cols // 2

    def whole(array):
        rank = array.ndim
        return pl.BlockSpec(array.shape, lambda i, sc: (0,) * rank)

    mine = pl.BlockSpec((1, half, chans), lambda i, sc: (i, sc[0], 0))
    kt_spec = pl.BlockSpec((1, 2, chans, cols), lambda i, sc: (i, 0, 0, 0))
    v_spec = pl.BlockSpec((1, 2, cols, chans), lambda i, sc: (i, 0, 0, 0))
    args = [q, *kts, *vs, sg, wo, osh, keys, *bounds, *blocks]
    in_specs = [mine, kt_spec, kt_spec, v_spec, v_spec, mine] + [whole(a) for a in args[6:]]
    kernel = functools.partial(attend_kernel, parts)
    aliases = {}
    if before is not None:
        args.append(before)
        in_specs.append(pl.BlockSpec(memory_space=pl.ANY))
        aliases = {len(args): 0}
    return pl.pallas_call(
        kernel,
        grid_spec=pltpu.PrefetchScalarGridSpec(
            num_scalar_prefetch=1,
            grid=(n,),
            in_specs=in_specs,
            out_specs=mine,
            scratch_shapes=[pltpu.VMEM((4, 4, half, 256), f32), pltpu.SMEM((1,), jnp.int32)],
        ),
        out_shape=jax.ShapeDtypeStruct((n, cols, chans), f32),
        input_output_aliases=aliases,
        compiler_params=pltpu.CompilerParams(vmem_limit_bytes=VMEM),
        cost_estimate=pl.CostEstimate(
            flops=2 * n * 4 * half * 1024 * 384, bytes_accessed=12 * 2**20, transcendentals=n * 4 * half * 1024
        ),
        name=name,
    )(sc, *args)


def local(pair, token_mask, ln_gain, ln_shift, w_qkvg, w_bias, gate_shift, w_out, out_shift):
    row, member = lax.axis_index("row"), lax.axis_index("head")
    yh, x, z = row // 32, (row // 8) % 4, row % 8

    g_hi = lax.reduce_precision(gate_shift, 8, 7)
    g_mid = lax.reduce_precision(gate_shift - g_hi, 8, 7)
    g_low = gate_shift - g_hi - g_mid
    g_rows = jnp.tile(jnp.stack([g_hi, g_mid, g_low]).astype(bf16), (1, 4))
    pack = jnp.concatenate([w_qkvg, w_out, g_rows, jnp.zeros((13, 128), bf16)], axis=0)
    packs = (pack, send(pack, to_core), send(pack, to_chip), send(pack, to_both))

    wb = jnp.concatenate([w_bias.T, jnp.zeros((12, 128), bf16)], axis=0)
    normed, chunk = norm_call(pair, ln_gain[None], ln_shift[None], wb)

    held = [send(chunk, spread(dy, dz)) for dy in range(2) for dz in range(2)]
    across = send(normed, to_chip)
    beside = send(normed, to_core)
    held = jnp.stack(held).reshape(2, 2, *chunk.shape)
    held = jnp.stack([held, send(held, along_z(1)), send(held, along_z(-1)), send(held, along_z(2))])
    left, right = send(held, along_x(1)), send(held, along_x(-1))
    behind_a, behind_b = send(left[:2], along_x(1)), send(right[2:], along_x(-1))

    q, sg, wo, kt_a, v_a, near = proj_call(True, normed, beside, packs)
    corner = send(across, to_core)
    kt_b, v_b, far = proj_call(False, across, corner, packs, q)

    quarters = jnp.where(token_mask == 1, 0.0, -1e9 * LOG2E).astype(f32).reshape(4, 1, 256)
    keys = jnp.stack([quarters[member ^ r] for r in range(4)])
    lo, hi = (x + 3) % 4, (x + 1) % 4
    common = [member, yh, z]
    osh = out_shift[None]
    sc_a = jnp.stack([1 - x % 2] + common + [lo // 2, hi // 2]).astype(jnp.int32)
    sc_b = jnp.stack([x % 2] + common + [x // 2, 1 - x // 2]).astype(jnp.int32)
    rest = (q, (kt_a, kt_b), (v_a, v_b), sg, wo, osh, keys, (near, far))
    done = attend_call(((4, 0), (5, 0)), sc_a, *rest, (left, right), None, "attend_far")
    return attend_call(
        ((4, 0), (5, 0), (5, 2)), sc_b, *rest, (held, behind_a, behind_b), done, "attend_near"
    )


def solution(mesh):
    placed = (
        P("row", "head", None),
        P(),
        P(),
        P(),
        P(None, "head"),
        P(),
        P("head"),
        P("head", None),
        P(),
    )
    return jax.shard_map(
        local, mesh=mesh, in_specs=placed, out_specs=P("row", "head", None), check_vma=False
    )
```
